1024 devices in a mesh: fsdp: 64 (over z, y), tp: 16 (over x, core).
Axes of the slice: x: 8, y: 8, z: 8, core: 2. Of those that a mesh axis runs over, the one named last changes fastest.
Arguments:
- momentum: float32 [8192, 28672], P('tp', 'fsdp'), may hold values from -16 to 16
- gradient: bfloat16 [8192, 28672], P('tp', 'fsdp'), may hold values from -40 to 40
- factor: float32 [28672, 512], P('fsdp'), may hold values from -6 to 6
Outputs:
- momentum_new: float32 [8192, 28672], P('tp', 'fsdp')
- factor_new: float32 [28672, 512], P('fsdp')
- update: bfloat16 [8192, 28672], P('tp', 'fsdp')
The draws below stay inside these ranges and needn't reach their ends.
All inputs are finite; a program needn't handle non-finite values.
Results may differ from the reference program's by a relative error of at most 0.005.
The reference program's roundings to bfloat16 on the way (of `blend_low`, `factor_low` and `left_low`) count: a program that leaves them out, or rounds other values in their place, can miss the bound.
Values may be sent and summed in bfloat16 or wider, within the bound.
No kernel may reach another device: no remote copies, remote signals or barrier semaphores. Data moves between devices by JAX's collectives and lax.ppermute only.
A program may use at most 32 MiB of HBM per device.

```python
import math
import jax
import jax.numpy as jnp
from jax import lax

D = 8192
FF = 28672
RANK = 512


def draw_gradient(key, part):
    key = jax.random.fold_in(key, 11)
    key_base, key_rows, key_cols = jax.random.split(key, 3)
    base_draw = 0.5 * jnp.clip(jax.random.normal(key_base, (D, FF), jnp.float32), -4.0, 4.0)
    row_scale = jnp.exp(jax.random.uniform(key_rows, (D, 1), jnp.float32, -1.15, 1.15))
    col_ramp = math.log(3.0) * (jnp.arange(FF, dtype=jnp.float32)[None, :] / FF - 0.5)
    col_scale = jnp.exp(jax.random.uniform(key_cols, (1, FF), jnp.float32, -1.15, 1.15) + col_ramp)
    values = base_draw * row_scale * col_scale
    return values.astype(jnp.bfloat16)


def spiked(array, stream_key, source, target, blocks, factor):
    owner, partner = [(jnp.arange(array.shape[dim]) // (array.shape[dim] // blocks)).reshape([-1 if axis == dim else 1 for axis in range(array.ndim)]) for dim in (source, target)]
    chosen = jax.random.permutation(stream_key, blocks)[partner]
    strong = (owner == chosen) | (owner == (partner + blocks // 2) % blocks)
    return jnp.where(strong, factor * array, array)


def block_levels(own_key, dims, shards, least, high):
    loudness, own = 1.0, jax.random.fold_in(own_key, 6)
    for position, shards_of in shards:
        heights = jnp.exp(jax.random.uniform(jax.random.fold_in(own, position), (shards_of,), jnp.float32, least / len(shards), high / len(shards)))
        loudness = loudness * jnp.repeat(heights, dims[position] // shards_of).reshape([-1 if axis == position else 1 for axis in range(len(dims))])
    return loudness


def scatter_about(own_key, shape, width, limit, pieces=(), held_as=jnp.bfloat16):
    gain = block_levels(own_key, shape, pieces, -0.22, 0.18) if pieces else 1.0
    entries = jax.random.normal(own_key, shape, jnp.float32) * width * gain
    return jnp.minimum(jnp.maximum(entries, -limit), limit).astype(held_as)


def heavy_noise(stream_key, dims, deviation, limit, pieces, heavy, held_as=jnp.bfloat16):
    result = deviation * jax.random.normal(stream_key, dims, jnp.float32)
    if pieces:
        result = result * block_levels(stream_key, dims, pieces, -0.22, 0.18)
    return jnp.clip(spiked(result, jax.random.fold_in(stream_key, 3), *heavy), -limit, limit).astype(held_as)


def setup_inputs(seed: int = 0) -> dict:
    key_of = jax.random.split(jax.random.key(seed), 4)
    momentum = heavy_noise(key_of[0], (D, FF), 1.0, 16.0, ((0, 16), (1, 64)), (1, 0, 64, 4.0), jnp.float32)
    gradient = draw_gradient(jax.random.fold_in(key_of[3], 71), 0)
    factor = scatter_about(key_of[2], (FF, RANK), 1.0, 6.0, ((0, 64),), jnp.float32)
    return {"momentum": momentum, "gradient": gradient, "factor": factor}


feedback = 0.05
epsilon = 1e-06

def reference(momentum, gradient, factor):
    blended = momentum + gradient.astype(jnp.float32)
    blend_low = blended.astype(jnp.bfloat16)
    factor_low = factor.astype(jnp.bfloat16)
    left = jnp.dot(blend_low.astype(jnp.float32), factor_low.astype(jnp.float32), preferred_element_type=jnp.float32)
    gram_sum = lax.dot_general(left.astype(jnp.float32), left.astype(jnp.float32), (((0,), (0,)), ((), ())), precision=lax.Precision.HIGHEST, preferred_element_type=jnp.float32)
    chol_lower = jnp.linalg.cholesky(gram_sum)
    left_low = lax.linalg.triangular_solve(chol_lower, left, left_side=False, lower=True, transpose_a=True).astype(jnp.bfloat16)
    right_full = lax.dot_general(blend_low.astype(jnp.float32), left_low.astype(jnp.float32), (((0,), (0,)), ((), ())), preferred_element_type=jnp.float32)
    col_scale = jnp.sqrt(lax.optimization_barrier(jnp.mean(right_full * right_full, axis=0)) + epsilon)
    factor_new = right_full / col_scale[None, :]
    feed_term = lax.dot_general(left_low.astype(jnp.float32), right_full.astype(jnp.bfloat16).astype(jnp.float32), (((1,), (1,)), ((), ())), preferred_element_type=jnp.float32)
    momentum_new = blended - feedback * feed_term
    update_full = lax.dot_general(left_low.astype(jnp.float32), factor_new.astype(jnp.bfloat16).astype(jnp.float32), (((1,), (1,)), ((), ())), preferred_element_type=jnp.float32)
    update = (math.sqrt(D / RANK) * update_full).astype(jnp.bfloat16)
    return (momentum_new, factor_new, update)
```

```python
import functools
import math

import jax
import jax.numpy as jnp
from jax import lax
from jax.experimental import pallas as pl
from jax.experimental.pallas import tpu as pltpu
from jax.sharding import Mesh, PartitionSpec as P

D = 8192
FF = 28672
RANK = 512
NB = 128
HALF = RANK // 2

feedback = 0.05
epsilon = 1e-06

ZY = ("z", "y")
EXACT = lax.Precision.HIGHEST
VMEM = pl.BlockSpec(memory_space=pltpu.VMEM)
SMEM = pl.BlockSpec(memory_space=pltpu.SMEM)
f32 = jnp.float32
bf16 = jnp.bfloat16


def dot(a, b, contract, precision=None):
    return lax.dot_general(
        a, b, (contract, ((), ())), precision=precision, preferred_element_type=f32
    )


def call(kernel, outs, *args, scratch=()):
    specs = [SMEM if a.dtype == jnp.int32 else VMEM for a in args]
    return pl.pallas_call(
        kernel,
        out_shape=outs,
        in_specs=specs,
        out_specs=jax.tree.map(lambda _: VMEM, outs),
        scratch_shapes=scratch,
        compiler_params=pltpu.CompilerParams(vmem_limit_bytes=40 * 2**20),
    )(*args)


def shape(dims, dtype):
    return jax.ShapeDtypeStruct(dims, dtype)


def gram_kernel(where_ref, left_ref, keep_ref, send_ref):
    left = left_ref[...]
    first = where_ref[0] * 8
    row = lax.broadcasted_iota(jnp.int32, (RANK, 8), 0)
    col = lax.broadcasted_iota(jnp.int32, (RANK, 8), 1)
    pick = jnp.where(row == first + col, 1.0, 0.0)
    columns = dot(left, pick, ((1,), (0,)), EXACT)
    rows = dot(columns, left, ((0,), (0,)), EXACT)
    own_low = where_ref[1] == 0
    low, high = rows[:, :HALF], rows[:, HALF:]
    keep_ref[...] = jnp.where(own_low, low, high)
    send_ref[...] = jnp.where(own_low, high, low)


def row_of(x, k):
    return jnp.broadcast_to(x[k : k + 1, :], (8, NB))


def lane_of(x, c):
    return jnp.broadcast_to(x[:, c : c + 1], (8, NB))


def diag_inverse(d):
    sub = lax.broadcasted_iota(jnp.int32, (8, NB), 0)
    lane = lax.broadcasted_iota(jnp.int32, (8, NB), 1)
    d = list(d)
    e = [jnp.where(lane == sub + 8 * i, 1.0, 0.0) for i in range(16)]
    out = []
    for t in range(16):
        s, g, f = d[t], e[t], e[t]
        cols = [lane_of(s, 8 * t + k) for k in range(8)]
        pivots = jnp.zeros((8, NB), f32)
        for k in range(8):
            own = sub == k
            pivot = row_of(cols[k], k)
            inv = 1.0 / pivot
            pivots = jnp.where(own, pivot, pivots)
            col = cols[k]
            for c in range(k + 1, 8):
                r = row_of(cols[c], k) * inv
                cols[c] = jnp.where(own, r, cols[c] - col * r)
            f = jnp.where(sub > k, f - col * (row_of(f, k) * inv), f)
            if t < 15:
                r = row_of(s, k) * inv
                s = jnp.where(own, r, s - col * r)
                r = row_of(g, k) * inv
                g = jnp.where(own, r, g - col * r)
        out.append(f * lax.rsqrt(pivots))
        for i in range(t + 1, 16):
            di, ei = d[i], e[i]
            u = [lane_of(d[i], 8 * t + k) for k in range(8)]
            for k in range(8):
                di = di - u[k] * row_of(s, k)
                ei = ei - u[k] * row_of(g, k)
            d[i], e[i] = di, ei
    return out


def ortho_kernel(
    where_ref, own_ref, other_ref, left_ref, mom_ref, grad_ref,
    q_ref, keep_ref, send_ref, a_ref, l_ref, w_ref,
):
    core = where_ref[1]
    a_ref[:, pl.ds(pl.multiple_of(core * HALF, HALF), HALF)] = own_ref[...]
    a_ref[:, pl.ds(pl.multiple_of((1 - core) * HALF, HALF), HALF)] = other_ref[...]
    l_ref[...] = left_ref[...]

    def outer(j, carry):
        j0 = pl.multiple_of(j * NB, NB)
        tiles = [
            a_ref[pl.ds(pl.multiple_of(j0 + 8 * i, 8), 8), pl.ds(j0, NB)]
            for i in range(16)
        ]
        for i, tile in enumerate(diag_inverse(tiles)):
            w_ref[8 * i : 8 * i + 8, :] = tile
        w = w_ref[...]
        panel = dot(w, a_ref[pl.ds(j0, NB), :], ((1,), (0,)), EXACT)
        lane = lax.broadcasted_iota(jnp.int32, (NB, RANK), 1)
        panel = jnp.where(lane >= j0 + NB, panel, 0.0)
        q = dot(l_ref[:, pl.ds(j0, NB)], w, ((1,), (1,)), EXACT)
        q_ref[:, pl.ds(j0, NB)] = q.astype(bf16)
        a_ref[...] -= dot(panel, panel, ((0,), (0,)), EXACT)
        l_ref[...] -= dot(q, panel, ((1,), (0,)), EXACT)
        return carry

    lax.fori_loop(0, RANK // NB, outer, 0)
    blend_low = (mom_ref[...] + grad_ref[...].astype(f32)).astype(bf16)
    right = dot(blend_low, q_ref[...], ((1,), (0,)))
    low, high = right[:, :HALF], right[:, HALF:]
    keep_ref[...] = jnp.where(core == 0, low, high)
    send_ref[...] = jnp.where(core == 0, high, low)


def whole(core, own_ref, other_ref):
    own, other = own_ref[...], other_ref[...]
    first = jnp.where(core == 0, own, other)
    second = jnp.where(core == 0, other, own)
    return jnp.concatenate([first, second], axis=1)


def momentum_kernel(where_ref, own_ref, other_ref, q_ref, mom_ref, grad_ref, out_ref, squares_ref):
    right = whole(where_ref[1], own_ref, other_ref)
    feed = dot(right, q_ref[...], ((1,), (1,)))
    out_ref[...] = mom_ref[...] + grad_ref[...].astype(f32) - feedback * feed
    wide = right.astype(f32)
    squares_ref[...] = jnp.sum(wide * wide, axis=0, keepdims=True)


def update_kernel(where_ref, own_ref, other_ref, q_ref, squares_ref, factor_ref, update_ref):
    right = whole(where_ref[1], own_ref, other_ref).astype(f32)
    mean = jnp.sum(squares_ref[...], axis=0, keepdims=True) / FF
    factor_new = right / jnp.sqrt(mean + epsilon)
    factor_ref[...] = factor_new
    update = dot(factor_new.astype(bf16), q_ref[...], ((1,), (1,)))
    update_ref[...] = (math.sqrt(D / RANK) * update).astype(bf16)


def to_all(x, axes, n):
    return lax.all_to_all(jnp.broadcast_to(x[None], (n,) + x.shape), axes, 0, 0)


def swap(x):
    return lax.ppermute(x, "core", [(0, 1), (1, 0)])


def per_device(nz, ny, nx, momentum, gradient, factor):
    n = nz * ny
    rows = momentum.shape[0] // n
    width = momentum.shape[1]
    blended = momentum + gradient.astype(f32)
    left_part = jnp.dot(
        blended.astype(bf16), factor.astype(bf16), preferred_element_type=f32
    )
    where = jnp.stack([lax.axis_index(ZY), lax.axis_index("core")]).astype(jnp.int32)
    mom_t, grad_t = momentum.T, gradient.T

    pieces = lax.all_to_all(left_part.reshape(n, rows, RANK), ZY, 0, 0)
    left = to_all(jnp.sum(pieces, axis=0), ZY, n).reshape(n * rows, RANK)

    keep, send = call(gram_kernel, (shape((8, HALF), f32),) * 2, where, left)
    gram_rows = jnp.sum(to_all(keep + swap(send), "x", nx), axis=0)
    gram_own = to_all(gram_rows, ZY, n).reshape(RANK, HALF)
    gram_other = swap(gram_own)

    left_low, keep, send = call(
        ortho_kernel,
        (shape(left.shape, bf16),) + (shape((width, HALF), f32),) * 2,
        where, gram_own, gram_other, left, mom_t, grad_t,
        scratch=[
            pltpu.VMEM((RANK, RANK), f32),
            pltpu.VMEM(left.shape, f32),
            pltpu.VMEM((NB, NB), f32),
        ],
    )
    part = (keep + swap(send)).reshape(nx, width // nx, HALF)
    mine = jnp.sum(lax.all_to_all(part, "x", 0, 0), axis=0).astype(bf16)
    own = to_all(mine, "x", nx).reshape(width, HALF)
    other = swap(own)

    momentum_t, squares = call(
        momentum_kernel,
        (shape((width, left.shape[0]), f32), shape((1, RANK), f32)),
        where, own, other, left_low, mom_t, grad_t,
    )
    squares = to_all(squares, ZY, n).reshape(n, RANK)
    factor_new, update_t = call(
        update_kernel,
        (shape((width, RANK), f32), shape((width, left.shape[0]), bf16)),
        where, own, other, left_low, squares,
    )
    return (momentum_t.T, factor_new, update_t.T)


def solution(mesh):
    nz = ny = math.isqrt(mesh.shape["fsdp"])
    nx = mesh.shape["tp"] // 2
    grid = Mesh(mesh.devices.reshape(nz, ny, nx, 2), ("z", "y", "x", "core"))
    tp = ("x", "core")
    return jax.shard_map(
        functools.partial(per_device, nz, ny, nx),
        mesh=grid,
        in_specs=(P(tp, ZY), P(tp, ZY), P(ZY, None)),
        out_specs=(P(tp, ZY), P(ZY, None), P(tp, ZY)),
        check_vma=False,
    )
```

```python
import functools
import math

import jax
import jax.numpy as jnp
from jax import lax
from jax.experimental import pallas as pl
from jax.experimental.pallas import tpu as pltpu
from jax.sharding import Mesh, PartitionSpec as P

D = 8192
FF = 28672
RANK = 512
NB = 64
TILE = 16
HALF = RANK // 2

feedback = 0.05
epsilon = 1e-06

ZY = ("z", "y")
EXACT = lax.Precision.HIGHEST
VMEM = pl.BlockSpec(memory_space=pltpu.VMEM)
SMEM = pl.BlockSpec(memory_space=pltpu.SMEM)
f32 = jnp.float32
bf16 = jnp.bfloat16
ORTHO_SCRATCH = [
    pltpu.VMEM((RANK, RANK), f32),
    pltpu.VMEM((RANK, RANK), f32),
    pltpu.VMEM((NB, 128), f32),
]


def dot(a, b, contract, precision=None):
    return lax.dot_general(
        a, b, (contract, ((), ())), precision=precision, preferred_element_type=f32
    )


def call(kernel, outs, *args, scratch=()):
    specs = [SMEM if a.dtype == jnp.int32 else VMEM for a in args]
    return pl.pallas_call(
        kernel,
        out_shape=outs,
        in_specs=specs,
        out_specs=jax.tree.map(lambda _: VMEM, outs),
        scratch_shapes=scratch,
        compiler_params=pltpu.CompilerParams(vmem_limit_bytes=40 * 2**20),
    )(*args)


def shape(dims, dtype):
    return jax.ShapeDtypeStruct(dims, dtype)


def gram_kernel(where_ref, left_ref, keep_ref, send_ref):
    left = left_ref[...]
    first = where_ref[0] * 8
    row = lax.broadcasted_iota(jnp.int32, (RANK, 8), 0)
    col = lax.broadcasted_iota(jnp.int32, (RANK, 8), 1)
    pick = jnp.where(row == first + col, 1.0, 0.0)
    columns = dot(left, pick, ((1,), (0,)), EXACT)
    rows = dot(columns, left, ((0,), (0,)), EXACT)
    own_low = where_ref[1] == 0
    low, high = rows[:, :HALF], rows[:, HALF:]
    keep_ref[...] = jnp.where(own_low, low, high)
    send_ref[...] = jnp.where(own_low, high, low)


def row_of(x, k):
    return jnp.broadcast_to(x[k : k + 1, :], x.shape)


def lane_of(x, c):
    return jnp.broadcast_to(x[:, c : c + 1], x.shape)


def diag_inverse(x, at):
    sub = lax.broadcasted_iota(jnp.int32, (TILE, 128), 0)
    x = list(x)
    out = []
    for t in range(len(x)):
        s = f = x[t]
        cols = [lane_of(s, at + TILE * t + k) for k in range(TILE)]
        pivots = jnp.zeros((TILE, 128), f32)
        for k in range(TILE):
            own = sub == k
            col = cols[k]
            pivot = row_of(col, k)
            inv = 1.0 / pivot
            pivots = jnp.where(own, pivot, pivots)
            for c in range(k + 1, TILE):
                r = row_of(cols[c], k)
                cols[c] = jnp.where(own, r * inv, cols[c] - (col * r) * inv)
            if k < TILE - 1:
                f = jnp.where(sub > k, f - col * (row_of(f, k) * inv), f)
            if t < len(x) - 1:
                r = row_of(s, k) * inv
                s = jnp.where(own, r, s - col * r)
        out.append(f * lax.rsqrt(pivots))
        for i in range(t + 1, len(x)):
            p = [lane_of(x[i], at + TILE * t + k) * row_of(s, k) for k in range(TILE)]
            while len(p) > 1:
                p = [p[m] + p[m + 1] for m in range(0, len(p), 2)]
            x[i] = x[i] - p[0]
    return out


def ortho_kernel(
    where_ref, own_ref, other_ref, left_ref, mom_ref, grad_ref,
    q_ref, keep_ref, send_ref, a_ref, l_ref, w_ref,
):
    core = where_ref[1]
    a_ref[:, pl.ds(pl.multiple_of(core * HALF, HALF), HALF)] = own_ref[...]
    a_ref[:, pl.ds(pl.multiple_of((1 - core) * HALF, HALF), HALF)] = other_ref[...]
    l_ref[...] = left_ref[...]
    sub = lax.broadcasted_iota(jnp.int32, (TILE, 128), 0)
    lane = lax.broadcasted_iota(jnp.int32, (TILE, 128), 1)

    for j in range(RANK // NB):
        j0 = j * NB
        base = j0 // 128 * 128
        at = j0 - base
        rest = 64 - at
        tiles = []
        for i in range(NB // TILE):
            a = a_ref[j0 + TILE * i : j0 + TILE * i + TILE, base : base + 128]
            eye = jnp.where(lane == rest + sub + TILE * i, 1.0, 0.0)
            tiles.append(jnp.where((lane >= at) & (lane < at + 64), a, eye))
        for i, tile in enumerate(diag_inverse(tiles, at)):
            w_ref[TILE * i : TILE * i + TILE, :] = tile
        w = w_ref[:, rest : rest + 64]
        if j + 1 < RANK // NB:
            c0 = (j0 + NB) // 128 * 128
            panel = dot(w, a_ref[j0 : j0 + NB, c0:], ((1,), (0,)), EXACT)
            if c0 < j0 + NB:
                wide = lax.broadcasted_iota(jnp.int32, panel.shape, 1)
                panel = jnp.where(wide >= j0 + NB - c0, panel, 0.0)
            a_ref[c0:, c0:] -= dot(panel, panel, ((0,), (0,)), EXACT)
        q = dot(l_ref[:, j0 : j0 + NB], w, ((1,), (1,)), EXACT)
        q_ref[:, j0 : j0 + NB] = q.astype(bf16)
        if j + 1 < RANK // NB:
            l_ref[:, c0:] -= dot(q, panel, ((1,), (0,)), EXACT)

    blend_low = (mom_ref[...] + grad_ref[...].astype(f32)).astype(bf16)
    right = dot(blend_low, q_ref[...], ((1,), (0,)))
    low, high = right[:, :HALF], right[:, HALF:]
    keep_ref[...] = jnp.where(core == 0, low, high)
    send_ref[...] = jnp.where(core == 0, high, low)


def whole(core, own_ref, other_ref):
    own, other = own_ref[...], other_ref[...]
    first = jnp.where(core == 0, own, other)
    second = jnp.where(core == 0, other, own)
    return jnp.concatenate([first, second], axis=1)


def momentum_kernel(where_ref, own_ref, other_ref, q_ref, mom_ref, grad_ref, out_ref, squares_ref):
    right = whole(where_ref[1], own_ref, other_ref)
    feed = dot(right, q_ref[...], ((1,), (1,)))
    out_ref[...] = mom_ref[...] + grad_ref[...].astype(f32) - feedback * feed
    wide = right.astype(f32)
    squares_ref[...] = jnp.sum(wide * wide, axis=0, keepdims=True)


def update_kernel(where_ref, own_ref, other_ref, q_ref, squares_ref, factor_ref, update_ref):
    right = whole(where_ref[1], own_ref, other_ref).astype(f32)
    mean = jnp.sum(squares_ref[...], axis=0, keepdims=True) / FF
    factor_new = right / jnp.sqrt(mean + epsilon)
    factor_ref[...] = factor_new
    update = dot(factor_new.astype(bf16), q_ref[...], ((1,), (1,)))
    update_ref[...] = (math.sqrt(D / RANK) * update).astype(bf16)


def to_all(x, axes, n):
    return lax.all_to_all(jnp.broadcast_to(x[None], (n,) + x.shape), axes, 0, 0)


def swap(x):
    return lax.ppermute(x, "core", [(0, 1), (1, 0)])


def per_device(nz, ny, nx, momentum, gradient, factor):
    n = nz * ny
    rows = momentum.shape[0] // n
    width = momentum.shape[1]
    blended = momentum + gradient.astype(f32)
    left_part = jnp.dot(
        blended.astype(bf16), factor.astype(bf16), preferred_element_type=f32
    )
    where = jnp.stack([lax.axis_index(ZY), lax.axis_index("core")]).astype(jnp.int32)
    where, left_part = lax.optimization_barrier((where, left_part))
    mom_t, grad_t = momentum.T, gradient.T

    pieces = lax.all_to_all(left_part.reshape(n, rows, RANK), ZY, 0, 0)
    left = to_all(jnp.sum(pieces, axis=0), ZY, n).reshape(n * rows, RANK)

    keep, send = call(gram_kernel, (shape((8, HALF), f32),) * 2, where, left)
    gram_rows = jnp.sum(to_all(keep + swap(send), "x", nx), axis=0)
    gram_own = to_all(gram_rows, ZY, n).reshape(RANK, HALF)
    gram_other = swap(gram_own)

    left_low, keep, send = call(
        ortho_kernel,
        (shape(left.shape, bf16),) + (shape((width, HALF), f32),) * 2,
        where, gram_own, gram_other, left, mom_t, grad_t,
        scratch=[
            pltpu.VMEM((RANK, RANK), f32),
            pltpu.VMEM(left.shape, f32),
            pltpu.VMEM((NB, 128), f32),
        ],
    )
    part = (keep + swap(send)).reshape(nx, width // nx, HALF)
    mine = jnp.sum(lax.all_to_all(part, "x", 0, 0), axis=0).astype(bf16)
    own = to_all(mine, "x", nx).reshape(width, HALF)
    other = swap(own)

    momentum_t, squares = call(
        momentum_kernel,
        (shape((width, left.shape[0]), f32), shape((1, RANK), f32)),
        where, own, other, left_low, mom_t, grad_t,
    )
    squares = to_all(squares, ZY, n).reshape(n, RANK)
    factor_new, update_t = call(
        update_kernel,
        (shape((width, RANK), f32), shape((width, left.shape[0]), bf16)),
        where, own, other, left_low, squares,
    )
    return (momentum_t.T, factor_new, update_t.T)


def solution(mesh):
    nz = ny = math.isqrt(mesh.shape["fsdp"])
    nx = mesh.shape["tp"] // 2
    grid = Mesh(mesh.devices.reshape(nz, ny, nx, 2), ("z", "y", "x", "core"))
    tp = ("x", "core")
    return jax.shard_map(
        functools.partial(per_device, nz, ny, nx),
        mesh=grid,
        in_specs=(P(tp, ZY), P(tp, ZY), P(ZY, None)),
        out_specs=(P(tp, ZY), P(ZY, None), P(tp, ZY)),
        check_vma=False,
    )
```

```python
import functools
import math

import jax
import jax.numpy as jnp
from jax import lax
from jax.experimental import pallas as pl
from jax.experimental.pallas import tpu as pltpu
from jax.sharding import Mesh, PartitionSpec as P

D = 8192
FF = 28672
RANK = 512
NB = 64
TILE = 16
HALF = RANK // 2

feedback = 0.05
epsilon = 1e-06

ZY = ("z", "y")
EXACT = lax.Precision.HIGHEST
VMEM = pl.BlockSpec(memory_space=pltpu.VMEM)
SMEM = pl.BlockSpec(memory_space=pltpu.SMEM)
f32 = jnp.float32
bf16 = jnp.bfloat16
ORTHO_SCRATCH = [
    pltpu.VMEM((RANK, RANK), f32),
    pltpu.VMEM((RANK, RANK), f32),
    pltpu.VMEM((NB, 128), f32),
]


def dot(a, b, contract, precision=None):
    return lax.dot_general(
        a, b, (contract, ((), ())), precision=precision, preferred_element_type=f32
    )


def call(kernel, outs, *args, scratch=()):
    specs = [SMEM if a.dtype == jnp.int32 else VMEM for a in args]
    return pl.pallas_call(
        kernel,
        out_shape=outs,
        in_specs=specs,
        out_specs=jax.tree.map(lambda _: VMEM, outs),
        scratch_shapes=scratch,
        compiler_params=pltpu.CompilerParams(vmem_limit_bytes=40 * 2**20),
    )(*args)


def shape(dims, dtype):
    return jax.ShapeDtypeStruct(dims, dtype)


def gram_kernel(where_ref, left_ref, halves_ref):
    left = left_ref[...]
    first = where_ref[0] * 8
    row = lax.broadcasted_iota(jnp.int32, (RANK, 8), 0)
    col = lax.broadcasted_iota(jnp.int32, (RANK, 8), 1)
    pick = jnp.where(row == first + col, 1.0, 0.0)
    columns = dot(left, pick, ((1,), (0,)), EXACT)
    rows = dot(columns, left, ((0,), (0,)), EXACT)
    halves_ref[0] = rows[:, :HALF]
    halves_ref[1] = rows[:, HALF:]


def row_of(x, k):
    return jnp.broadcast_to(x[k : k + 1, :], x.shape)


def lane_of(x, c):
    return jnp.broadcast_to(x[:, c : c + 1], x.shape)


def diag_inverse(x, at):
    sub = lax.broadcasted_iota(jnp.int32, (TILE, 128), 0)
    x = list(x)
    out = []
    for t in range(len(x)):
        s = f = x[t]
        cols = [lane_of(s, at + TILE * t + k) for k in range(TILE)]
        pivots = jnp.zeros((TILE, 128), f32)
        for k in range(TILE):
            own = sub == k
            col = cols[k]
            pivot = row_of(col, k)
            inv = 1.0 / pivot
            pivots = jnp.where(own, pivot, pivots)
            for c in range(k + 1, TILE):
                r = row_of(cols[c], k)
                cols[c] = jnp.where(own, r * inv, cols[c] - (col * r) * inv)
            if k < TILE - 1:
                f = jnp.where(sub > k, f - col * (row_of(f, k) * inv), f)
            if t < len(x) - 1:
                r = row_of(s, k) * inv
                s = jnp.where(own, r, s - col * r)
        out.append(f * lax.rsqrt(pivots))
        for i in range(t + 1, len(x)):
            p = [lane_of(x[i], at + TILE * t + k) * row_of(s, k) for k in range(TILE)]
            while len(p) > 1:
                p = [p[m] + p[m + 1] for m in range(0, len(p), 2)]
            x[i] = x[i] - p[0]
    return out


def ortho_kernel(
    where_ref, own_ref, other_ref, left_ref, mom_ref, grad_ref,
    q_ref, keep_ref, send_ref, a_ref, l_ref, w_ref,
):
    core = where_ref[1]
    a_ref[:, pl.ds(pl.multiple_of(core * HALF, HALF), HALF)] = own_ref[...]
    a_ref[:, pl.ds(pl.multiple_of((1 - core) * HALF, HALF), HALF)] = other_ref[...]
    l_ref[...] = left_ref[...]
    sub = lax.broadcasted_iota(jnp.int32, (TILE, 128), 0)
    lane = lax.broadcasted_iota(jnp.int32, (TILE, 128), 1)

    for j in range(RANK // NB):
        j0 = j * NB
        base = j0 // 128 * 128
        at = j0 - base
        rest = 64 - at
        tiles = []
        for i in range(NB // TILE):
            a = a_ref[j0 + TILE * i : j0 + TILE * i + TILE, base : base + 128]
            eye = jnp.where(lane == rest + sub + TILE * i, 1.0, 0.0)
            tiles.append(jnp.where((lane >= at) & (lane < at + 64), a, eye))
        for i, tile in enumerate(diag_inverse(tiles, at)):
            w_ref[TILE * i : TILE * i + TILE, :] = tile
        w = w_ref[:, rest : rest + 64]
        if j + 1 < RANK // NB:
            c0 = (j0 + NB) // 128 * 128
            panel = dot(w, a_ref[j0 : j0 + NB, c0:], ((1,), (0,)), EXACT)
            if c0 < j0 + NB:
                wide = lax.broadcasted_iota(jnp.int32, panel.shape, 1)
                panel = jnp.where(wide >= j0 + NB - c0, panel, 0.0)
            a_ref[c0:, c0:] -= dot(panel, panel, ((0,), (0,)), EXACT)
        q = dot(l_ref[:, j0 : j0 + NB], w, ((1,), (1,)), EXACT)
        q_ref[:, j0 : j0 + NB] = q.astype(bf16)
        if j + 1 < RANK // NB:
            l_ref[:, c0:] -= dot(q, panel, ((1,), (0,)), EXACT)

    blend_low = (mom_ref[...] + grad_ref[...].astype(f32)).astype(bf16)
    right = dot(blend_low, q_ref[...], ((1,), (0,)))
    low, high = right[:, :HALF], right[:, HALF:]
    keep_ref[...] = jnp.where(core == 0, low, high)
    send_ref[...] = jnp.where(core == 0, high, low)


def momentum_kernel(right_ref, q_ref, mom_ref, grad_ref, out_ref, squares_ref):
    right = right_ref[...]
    feed = dot(right.astype(bf16), q_ref[...], ((1,), (1,)))
    out_ref[...] = mom_ref[...] + grad_ref[...].astype(f32) - feedback * feed
    squares_ref[...] = jnp.sum(right * right, axis=0, keepdims=True)


def update_kernel(right_ref, q_ref, squares_ref, factor_ref, update_ref):
    mean = jnp.sum(squares_ref[...], axis=0, keepdims=True) / FF
    factor_new = right_ref[...] / jnp.sqrt(mean + epsilon)
    factor_ref[...] = factor_new
    update = dot(factor_new.astype(bf16), q_ref[...], ((1,), (1,)))
    update_ref[...] = (math.sqrt(D / RANK) * update).astype(bf16)


def enc(x, scale, knee):
    x = x * scale
    size = jnp.abs(x)
    root = jnp.sqrt(size * knee)
    return jnp.where(size < knee, jnp.where(x < 0, -root, root), x).astype(jnp.float16)


def dec(x, scale, knee):
    x = x.astype(f32)
    size = jnp.abs(x)
    return jnp.where(size < knee, x * size * (1.0 / knee), x) * (1.0 / scale)


PART = (2.0**-2, 0.25)
LEFT = (2.0**-8, 0.125)
RIGHT = (2.0**3, 0.25)


def to_all(x, axes, n):
    return lax.all_to_all(jnp.broadcast_to(x[None], (n,) + x.shape), axes, 0, 0)


def swap(x):
    return lax.ppermute(x, "core", [(0, 1), (1, 0)])


def per_device(nz, ny, nx, momentum, gradient, factor):
    n = nz * ny
    rows = momentum.shape[0] // n
    width = momentum.shape[1]
    blended = momentum + gradient.astype(f32)
    left_part = jnp.dot(
        blended.astype(bf16), factor.astype(bf16), preferred_element_type=f32
    )
    core = lax.axis_index("core")
    where = jnp.stack([lax.axis_index(ZY), core]).astype(jnp.int32)
    where, left_part = lax.optimization_barrier((where, left_part))
    mom_t, grad_t = momentum.T, gradient.T

    pieces = lax.all_to_all(enc(left_part, *PART).reshape(n, rows, RANK), ZY, 0, 0)
    share = enc(jnp.sum(dec(pieces, *PART), axis=0), *LEFT)
    left = dec(to_all(share, ZY, n), *LEFT).reshape(n * rows, RANK)

    halves = call(gram_kernel, shape((2, 8, HALF), f32), where, left)
    halves = jnp.broadcast_to(halves[None], (nx, 2, 8, HALF)).reshape(2 * nx, 8, HALF)
    gram_rows = jnp.sum(lax.all_to_all(halves, ("x", "core"), 0, 0), axis=0)
    gram_own = to_all(gram_rows, ZY, n).reshape(RANK, HALF)
    gram_other = swap(gram_own)

    left_low, keep, send = call(
        ortho_kernel,
        (shape(left.shape, bf16),) + (shape((width, HALF), f32),) * 2,
        where, gram_own, gram_other, left, mom_t, grad_t,
        scratch=ORTHO_SCRATCH,
    )
    part = enc(keep + swap(send), *RIGHT).reshape(nx, width // nx, HALF)
    mine = jnp.sum(dec(lax.all_to_all(part, "x", 0, 0), *RIGHT), axis=0)
    own = to_all(enc(mine, *RIGHT), "x", nx).reshape(width, HALF)
    other = swap(own)
    low = jnp.where(core == 0, own, other)
    high = jnp.where(core == 0, other, own)
    right = dec(jnp.concatenate([low, high], axis=1), *RIGHT)

    momentum_t, squares = call(
        momentum_kernel,
        (shape((width, left.shape[0]), f32), shape((1, RANK), f32)),
        right, left_low, mom_t, grad_t,
    )
    squares = to_all(squares, ZY, n).reshape(n, RANK)
    factor_new, update_t = call(
        update_kernel,
        (shape((width, RANK), f32), shape((width, left.shape[0]), bf16)),
        right, left_low, squares,
    )
    return (momentum_t.T, factor_new, update_t.T)


def solution(mesh):
    nz = ny = math.isqrt(mesh.shape["fsdp"])
    nx = mesh.shape["tp"] // 2
    grid = Mesh(mesh.devices.reshape(nz, ny, nx, 2), ("z", "y", "x", "core"))
    tp = ("x", "core")
    return jax.shard_map(
        functools.partial(per_device, nz, ny, nx),
        mesh=grid,
        in_specs=(P(tp, ZY), P(tp, ZY), P(ZY, None)),
        out_specs=(P(tp, ZY), P(ZY, None), P(tp, ZY)),
        check_vma=False,
    )
```

```python
import functools
import math

import jax
import jax.numpy as jnp
from jax import lax
from jax.experimental import pallas as pl
from jax.experimental.pallas import tpu as pltpu
from jax.sharding import Mesh, PartitionSpec as P

D = 8192
FF = 28672
RANK = 512
NB = 64
TILE = 16
HALF = RANK // 2

feedback = 0.05
epsilon = 1e-06

ZY = ("z", "y")
EXACT = lax.Precision.HIGHEST
VMEM = pl.BlockSpec(memory_space=pltpu.VMEM)
SMEM = pl.BlockSpec(memory_space=pltpu.SMEM)
f32 = jnp.float32
bf16 = jnp.bfloat16
ORTHO_SCRATCH = [
    pltpu.VMEM((RANK, RANK), f32),
    pltpu.VMEM((RANK, RANK), f32),
    pltpu.VMEM((NB, 128), f32),
]


def dot(a, b, contract, precision=None):
    return lax.dot_general(
        a, b, (contract, ((), ())), precision=precision, preferred_element_type=f32
    )


def call(kernel, outs, *args, scratch=()):
    specs = [SMEM if a.dtype == jnp.int32 else VMEM for a in args]
    return pl.pallas_call(
        kernel,
        out_shape=outs,
        in_specs=specs,
        out_specs=jax.tree.map(lambda _: VMEM, outs),
        scratch_shapes=scratch,
        compiler_params=pltpu.CompilerParams(vmem_limit_bytes=40 * 2**20),
    )(*args)


def shape(dims, dtype):
    return jax.ShapeDtypeStruct(dims, dtype)


def gram_kernel(where_ref, left_ref, halves_ref, turned_ref):
    group, first = where_ref[0] // 16, where_ref[0] % 16 * 8
    turned_ref[...] = left_ref[:, pl.ds(pl.multiple_of(group * 128, 128), 128)].T
    columns = turned_ref[pl.ds(pl.multiple_of(first, 8), 8), :]
    rows = dot(columns, left_ref[...], ((1,), (0,)), EXACT)
    halves_ref[0] = rows[:, :HALF]
    halves_ref[1] = rows[:, HALF:]


def row_of(x, k):
    return jnp.broadcast_to(x[k // 8][k % 8 : k % 8 + 1, :], (8, 128))


def lane_of(x, c):
    return [jnp.broadcast_to(h[:, c : c + 1], (8, 128)) for h in x]


def diag_inverse(x, at, fill=None):
    sub = lax.broadcasted_iota(jnp.int32, (8, 128), 0)
    x = list(x)
    out = []

    def below(old, m, r, k, done):
        new = [h - a * r for h, a in zip(old, m)]
        new[k // 8] = jnp.where(sub == k % 8, done, new[k // 8])
        return new

    for t in range(len(x)):
        s = f = x[t]
        cols = [lane_of(s, at + TILE * t + k) for k in range(TILE)]
        pivots = [jnp.zeros((8, 128), f32)] * 2
        for k in range(TILE):
            col = cols[k]
            pivot = row_of(col, k)
            inv = 1.0 / pivot
            pivots[k // 8] = jnp.where(sub == k % 8, pivot, pivots[k // 8])
            m = [h * inv for h in col]
            for c in range(k + 1, TILE):
                r = row_of(cols[c], k)
                if c == k + 1:
                    new = [h - (a * r) * inv for h, a in zip(cols[c], col)]
                    new[k // 8] = jnp.where(sub == k % 8, r * inv, new[k // 8])
                    cols[c] = new
                else:
                    cols[c] = below(cols[c], m, r, k, r * inv)
            if k < TILE - 1:
                r = row_of(f, k)
                new = list(f)
                if k < 7:
                    new[0] = jnp.where(sub > k, f[0] - m[0] * r, f[0])
                if k < 8:
                    new[1] = f[1] - m[1] * r
                else:
                    new[1] = jnp.where(sub > k - 8, f[1] - m[1] * r, f[1])
                f = new
            if t < len(x) - 1:
                r = row_of(s, k)
                s = below(s, m, r, k, r * inv)
        out += [h * lax.rsqrt(p) for h, p in zip(f, pivots)]
        if t == 0 and fill is not None:
            fill()
        for i in range(t + 1, len(x)):
            u = [lane_of(x[i], at + TILE * t + k) for k in range(TILE)]
            r = [row_of(s, k) for k in range(TILE)]
            new = []
            for h in range(2):
                p = [u[k][h] * r[k] for k in range(TILE)]
                while len(p) > 1:
                    p = [p[n] + p[n + 1] for n in range(0, len(p), 2)]
                new.append(x[i][h] - p[0])
            x[i] = new
    return out


def ortho_kernel(
    where_ref, own_ref, other_ref, left_ref, mom_ref, grad_ref,
    q_ref, keep_ref, send_ref, a_ref, l_ref, w_ref,
):
    core = where_ref[1]
    a_ref[:, pl.ds(pl.multiple_of(core * HALF, HALF), HALF)] = own_ref[...]
    a_ref[:, pl.ds(pl.multiple_of((1 - core) * HALF, HALF), HALF)] = other_ref[...]
    l_ref[...] = left_ref[...]
    sub = lax.broadcasted_iota(jnp.int32, (8, 128), 0)
    lane = lax.broadcasted_iota(jnp.int32, (8, 128), 1)

    fill = None
    steps = RANK // NB
    for j in range(steps):
        j0 = j * NB
        base = j0 // 128 * 128
        at = j0 - base
        rest = 64 - at
        tiles = []
        for i in range(NB // 8):
            a = a_ref[j0 + 8 * i : j0 + 8 * i + 8, base : base + 128]
            eye = jnp.where(lane == rest + sub + 8 * i, 1.0, 0.0)
            tiles.append(jnp.where((lane >= at) & (lane < at + 64), a, eye))
        tiles = [tiles[i : i + 2] for i in range(0, NB // 8, 2)]
        for i, tile in enumerate(diag_inverse(tiles, at, fill)):
            w_ref[8 * i : 8 * i + 8, :] = tile
        w = w_ref[:, rest : rest + 64]
        panel, c0 = None, RANK
        jn = j0 + NB
        if j + 1 < steps:
            c0 = jn // 128 * 128
            panel = dot(w, a_ref[j0 : j0 + NB, c0:], ((1,), (0,)), EXACT)
            if c0 < jn:
                wide = lax.broadcasted_iota(jnp.int32, panel.shape, 1)
                panel = jnp.where(wide >= jn - c0, panel, 0.0)
            ahead = panel[:, jn - c0 : jn - c0 + NB]
            a_ref[jn : jn + NB, c0:] -= dot(ahead, panel, ((0,), (0,)), EXACT)

        def fill(j0=j0, w=w, panel=panel, c0=c0, jn=jn):
            if jn + NB < RANK:
                c1 = (jn + NB) // 128 * 128
                below, right = panel[:, jn + NB - c0 :], panel[:, c1 - c0 :]
                a_ref[jn + NB :, c1:] -= dot(below, right, ((0,), (0,)), EXACT)
            q = dot(l_ref[:, j0 : j0 + NB], w, ((1,), (1,)), EXACT)
            q_ref[:, j0 : j0 + NB] = q.astype(bf16)
            if panel is not None:
                l_ref[:, c0:] -= dot(q, panel, ((1,), (0,)), EXACT)

    fill()
    blend_low = (mom_ref[...] + grad_ref[...].astype(f32)).astype(bf16)
    right = dot(blend_low, q_ref[...], ((1,), (0,)))
    low, high = right[:, :HALF], right[:, HALF:]
    keep_ref[...] = jnp.where(core == 0, low, high)
    send_ref[...] = jnp.where(core == 0, high, low)


def momentum_kernel(right_ref, q_ref, mom_ref, grad_ref, out_ref, squares_ref):
    right = right_ref[...]
    feed = dot(right.astype(bf16), q_ref[...], ((1,), (1,)))
    out_ref[...] = mom_ref[...] + grad_ref[...].astype(f32) - feedback * feed
    squares_ref[...] = jnp.sum(right * right, axis=0, keepdims=True)


def update_kernel(right_ref, q_ref, squares_ref, factor_ref, update_ref):
    mean = jnp.sum(squares_ref[...], axis=0, keepdims=True) / FF
    factor_new = right_ref[...] / jnp.sqrt(mean + epsilon)
    factor_ref[...] = factor_new
    update = dot(factor_new.astype(bf16), q_ref[...], ((1,), (1,)))
    update_ref[...] = (math.sqrt(D / RANK) * update).astype(bf16)


def enc(x, scale, knee):
    x = x * scale
    size = jnp.abs(x)
    root = jnp.sqrt(size * knee)
    return jnp.where(size < knee, jnp.where(x < 0, -root, root), x).astype(jnp.float16)


def dec(x, scale, knee):
    x = x.astype(f32)
    size = jnp.abs(x)
    return jnp.where(size < knee, x * size * (1.0 / knee), x) * (1.0 / scale)


PART = (2.0**-2, 0.25)
LEFT = (2.0**-8, 0.125)
RIGHT = (2.0**3, 0.25)


def to_all(x, axes, n):
    return lax.all_to_all(jnp.broadcast_to(x[None], (n,) + x.shape), axes, 0, 0)


def swap(x):
    return lax.ppermute(x, "core", [(0, 1), (1, 0)])


def per_device(nz, ny, nx, momentum, gradient, factor):
    n = nz * ny
    rows = momentum.shape[0] // n
    width = momentum.shape[1]
    blended = momentum + gradient.astype(f32)
    left_part = jnp.dot(
        blended.astype(bf16), factor.astype(bf16), preferred_element_type=f32
    )
    core = lax.axis_index("core")
    where = jnp.stack([lax.axis_index(ZY), core]).astype(jnp.int32)
    where, left_part = lax.optimization_barrier((where, left_part))
    mom_t, grad_t = momentum.T, gradient.T

    pieces = lax.all_to_all(enc(left_part, *PART).reshape(n, rows, RANK), ZY, 0, 0)
    share = enc(jnp.sum(dec(pieces, *PART), axis=0), *LEFT)
    left = dec(to_all(share, ZY, n), *LEFT).reshape(n * rows, RANK)

    halves = call(
        gram_kernel, shape((2, 8, HALF), f32), where, left,
        scratch=[pltpu.VMEM((128, left.shape[0]), f32)],
    )
    halves = jnp.broadcast_to(halves[None], (nx, 2, 8, HALF)).reshape(2 * nx, 8, HALF)
    gram_rows = jnp.sum(lax.all_to_all(halves, ("x", "core"), 0, 0), axis=0)
    gram_own = to_all(gram_rows, ZY, n).reshape(RANK, HALF)
    gram_other = swap(gram_own)

    left_low, keep, send = call(
        ortho_kernel,
        (shape(left.shape, bf16),) + (shape((width, HALF), f32),) * 2,
        where, gram_own, gram_other, left, mom_t, grad_t,
        scratch=ORTHO_SCRATCH,
    )
    part = enc(keep + swap(send), *RIGHT).reshape(nx, width // nx, HALF)
    mine = jnp.sum(dec(lax.all_to_all(part, "x", 0, 0), *RIGHT), axis=0)
    own = to_all(enc(mine, *RIGHT), "x", nx).reshape(width, HALF)
    other = swap(own)
    low = jnp.where(core == 0, own, other)
    high = jnp.where(core == 0, other, own)
    right = dec(jnp.concatenate([low, high], axis=1), *RIGHT)

    momentum_t, squares = call(
        momentum_kernel,
        (shape((width, left.shape[0]), f32), shape((1, RANK), f32)),
        right, left_low, mom_t, grad_t,
    )
    squares = to_all(squares, ZY, n).reshape(n, RANK)
    factor_new, update_t = call(
        update_kernel,
        (shape((width, RANK), f32), shape((width, left.shape[0]), bf16)),
        right, left_low, squares,
    )
    return (momentum_t.T, factor_new, update_t.T)


def solution(mesh):
    nz = ny = math.isqrt(mesh.shape["fsdp"])
    nx = mesh.shape["tp"] // 2
    grid = Mesh(mesh.devices.reshape(nz, ny, nx, 2), ("z", "y", "x", "core"))
    tp = ("x", "core")
    return jax.shard_map(
        functools.partial(per_device, nz, ny, nx),
        mesh=grid,
        in_specs=(P(tp, ZY), P(tp, ZY), P(ZY, None)),
        out_specs=(P(tp, ZY), P(ZY, None), P(tp, ZY)),
        check_vma=False,
    )
```

```python
import functools
import math

import jax
import jax.numpy as jnp
from jax import lax
from jax.experimental import pallas as pl
from jax.experimental.pallas import tpu as pltpu
from jax.sharding import Mesh, PartitionSpec as P

D = 8192
FF = 28672
RANK = 512
NB = 64
TILE = 16
HALF = RANK // 2

feedback = 0.05
epsilon = 1e-06

ZY = ("z", "y")
EXACT = lax.Precision.HIGHEST
VMEM = pl.BlockSpec(memory_space=pltpu.VMEM)
SMEM = pl.BlockSpec(memory_space=pltpu.SMEM)
f32 = jnp.float32
bf16 = jnp.bfloat16
ORTHO_SCRATCH = [
    pltpu.VMEM((RANK, RANK), f32),
    pltpu.VMEM((RANK, RANK), f32),
    pltpu.VMEM((NB, 128), f32),
]


def dot(a, b, contract, precision=None):
    return lax.dot_general(
        a, b, (contract, ((), ())), precision=precision, preferred_element_type=f32
    )


def call(kernel, outs, *args, scratch=()):
    specs = [SMEM if a.dtype == jnp.int32 else VMEM for a in args]
    return pl.pallas_call(
        kernel,
        out_shape=outs,
        in_specs=specs,
        out_specs=jax.tree.map(lambda _: VMEM, outs),
        scratch_shapes=scratch,
        compiler_params=pltpu.CompilerParams(vmem_limit_bytes=40 * 2**20),
    )(*args)


def shape(dims, dtype):
    return jax.ShapeDtypeStruct(dims, dtype)


def gram_kernel(where_ref, left_ref, halves_ref, turned_ref):
    group, first = where_ref[0] // 16, where_ref[0] % 16 * 8
    turned_ref[...] = left_ref[:, pl.ds(pl.multiple_of(group * 128, 128), 128)].T
    columns = turned_ref[pl.ds(pl.multiple_of(first, 8), 8), :]
    rows = dot(columns, left_ref[...], ((1,), (0,)), EXACT)
    halves_ref[0] = rows[:, :HALF]
    halves_ref[1] = rows[:, HALF:]


def row_of(x, k):
    return jnp.broadcast_to(x[k // 8][k % 8 : k % 8 + 1, :], (8, 128))


def lane_of(x, c):
    return [jnp.broadcast_to(h[:, c : c + 1], (8, 128)) for h in x]


def diag_inverse(x, at, fill=None):
    sub = lax.broadcasted_iota(jnp.int32, (8, 128), 0)
    x = list(x)
    out = []

    def below(old, m, r, k, done):
        new = [h - a * r for h, a in zip(old, m)]
        new[k // 8] = jnp.where(sub == k % 8, done, new[k // 8])
        return new

    for t in range(len(x)):
        s = f = x[t]
        cols = [lane_of(s, at + TILE * t + k) for k in range(TILE)]
        pivots = [jnp.zeros((8, 128), f32)] * 2
        for k in range(TILE):
            col = cols[k]
            pivot = row_of(col, k)
            inv = 1.0 / pivot
            pivots[k // 8] = jnp.where(sub == k % 8, pivot, pivots[k // 8])
            m = [h * inv for h in col]
            for c in range(k + 1, TILE):
                r = row_of(cols[c], k)
                if c == k + 1:
                    new = [h - (a * r) * inv for h, a in zip(cols[c], col)]
                    new[k // 8] = jnp.where(sub == k % 8, r * inv, new[k // 8])
                    cols[c] = new
                else:
                    cols[c] = below(cols[c], m, r, k, r * inv)
            if k < TILE - 1:
                r = row_of(f, k)
                new = list(f)
                if k < 7:
                    new[0] = jnp.where(sub > k, f[0] - m[0] * r, f[0])
                if k < 8:
                    new[1] = f[1] - m[1] * r
                else:
                    new[1] = jnp.where(sub > k - 8, f[1] - m[1] * r, f[1])
                f = new
            if t < len(x) - 1:
                r = row_of(s, k)
                s = below(s, m, r, k, r * inv)
        out += [h * lax.rsqrt(p) for h, p in zip(f, pivots)]
        if t == 0 and fill is not None:
            fill()
        for i in range(t + 1, len(x)):
            u = [lane_of(x[i], at + TILE * t + k) for k in range(TILE)]
            r = [row_of(s, k) for k in range(TILE)]
            new = []
            for h in range(2):
                p = [u[k][h] * r[k] for k in range(TILE)]
                while len(p) > 1:
                    p = [p[n] + p[n + 1] for n in range(0, len(p), 2)]
                new.append(x[i][h] - p[0])
            x[i] = new
    return out


def ortho_kernel(
    where_ref, own_ref, other_ref, left_ref, mom_ref, grad_ref,
    q_ref, keep_ref, send_ref, a_ref, l_ref, w_ref,
):
    core = where_ref[1]
    a_ref[:, pl.ds(pl.multiple_of(core * HALF, HALF), HALF)] = own_ref[...]
    a_ref[:, pl.ds(pl.multiple_of((1 - core) * HALF, HALF), HALF)] = other_ref[...]
    l_ref[...] = left_ref[...]
    sub = lax.broadcasted_iota(jnp.int32, (8, 128), 0)
    lane = lax.broadcasted_iota(jnp.int32, (8, 128), 1)

    fill = None
    steps = RANK // NB
    for j in range(steps):
        j0 = j * NB
        base = j0 // 128 * 128
        at = j0 - base
        rest = 64 - at
        tiles = []
        for i in range(NB // 8):
            a = a_ref[j0 + 8 * i : j0 + 8 * i + 8, base : base + 128]
            eye = jnp.where(lane == rest + sub + 8 * i, 1.0, 0.0)
            tiles.append(jnp.where((lane >= at) & (lane < at + 64), a, eye))
        tiles = [tiles[i : i + 2] for i in range(0, NB // 8, 2)]
        for i, tile in enumerate(diag_inverse(tiles, at, fill)):
            w_ref[8 * i : 8 * i + 8, :] = tile
        w = w_ref[:, rest : rest + 64]
        panel, c0 = None, RANK
        jn = j0 + NB
        if j + 1 < steps:
            c0 = jn // 128 * 128
            panel = dot(w, a_ref[j0 : j0 + NB, c0:], ((1,), (0,)), EXACT)
            if c0 < jn:
                wide = lax.broadcasted_iota(jnp.int32, panel.shape, 1)
                panel = jnp.where(wide >= jn - c0, panel, 0.0)
            ahead = panel[:, jn - c0 : jn - c0 + NB]
            a_ref[jn : jn + NB, c0:] -= dot(ahead, panel, ((0,), (0,)), EXACT)

        def fill(j0=j0, w=w, panel=panel, c0=c0, jn=jn):
            if jn + NB < RANK:
                c1 = (jn + NB) // 128 * 128
                below, right = panel[:, jn + NB - c0 :], panel[:, c1 - c0 :]
                a_ref[jn + NB :, c1:] -= dot(below, right, ((0,), (0,)), EXACT)
            q = dot(l_ref[:, j0 : j0 + NB], w, ((1,), (1,)), EXACT)
            q_ref[:, j0 : j0 + NB] = q.astype(bf16)
            if panel is not None:
                l_ref[:, c0:] -= dot(q, panel, ((1,), (0,)), EXACT)

    fill()
    blend_low = (mom_ref[...] + grad_ref[...].astype(f32)).astype(bf16)
    right = dot(blend_low, q_ref[...], ((1,), (0,)))
    low, high = right[:, :HALF], right[:, HALF:]
    keep_ref[...] = jnp.where(core == 0, low, high)
    send_ref[...] = jnp.where(core == 0, high, low)


def momentum_kernel(right_ref, q_ref, mom_ref, grad_ref, out_ref):
    feed = dot(right_ref[...].astype(bf16), q_ref[...], ((1,), (1,)))
    out_ref[...] = mom_ref[...] + grad_ref[...].astype(f32) - feedback * feed


def update_kernel(right_ref, q_ref, squares_ref, factor_ref, update_ref):
    mean = jnp.sum(squares_ref[...], axis=0, keepdims=True) / FF
    factor_new = right_ref[...] / jnp.sqrt(mean + epsilon)
    factor_ref[...] = factor_new
    update = dot(factor_new.astype(bf16), q_ref[...], ((1,), (1,)))
    update_ref[...] = (math.sqrt(D / RANK) * update).astype(bf16)


def enc(x, scale, knee):
    x = x * scale
    size = jnp.abs(x)
    root = jnp.sqrt(size * knee)
    return jnp.where(size < knee, jnp.where(x < 0, -root, root), x).astype(jnp.float16)


def dec(x, scale, knee):
    x = x.astype(f32)
    size = jnp.abs(x)
    return jnp.where(size < knee, x * size * (1.0 / knee), x) * (1.0 / scale)


PART = (2.0**-2, 0.25)
LEFT = (2.0**-8, 0.125)
RIGHT = (2.0**3, 0.25)


def to_all(x, axes, n):
    return lax.all_to_all(jnp.broadcast_to(x[None], (n,) + x.shape), axes, 0, 0)


def swap(x):
    return lax.ppermute(x, "core", [(0, 1), (1, 0)])


def per_device(nz, ny, nx, momentum, gradient, factor):
    n = nz * ny
    rows = momentum.shape[0] // n
    width = momentum.shape[1]
    blended = momentum + gradient.astype(f32)
    left_part = jnp.dot(
        blended.astype(bf16), factor.astype(bf16), preferred_element_type=f32
    )
    core = lax.axis_index("core")
    where = jnp.stack([lax.axis_index(ZY), core]).astype(jnp.int32)
    where, left_part = lax.optimization_barrier((where, left_part))
    mom_t, grad_t = momentum.T, gradient.T

    pieces = lax.all_to_all(enc(left_part, *PART).reshape(n, rows, RANK), ZY, 0, 0)
    share = enc(jnp.sum(dec(pieces, *PART), axis=0), *LEFT)
    left = dec(to_all(share, ZY, n), *LEFT).reshape(n * rows, RANK)

    halves = call(
        gram_kernel, shape((2, 8, HALF), f32), where, left,
        scratch=[pltpu.VMEM((128, left.shape[0]), f32)],
    )
    halves = jnp.broadcast_to(halves[None], (nx, 2, 8, HALF)).reshape(2 * nx, 8, HALF)
    gram_rows = jnp.sum(lax.all_to_all(halves, ("x", "core"), 0, 0), axis=0)
    gram_own = to_all(gram_rows, ZY, n).reshape(RANK, HALF)
    gram_other = swap(gram_own)

    left_low, keep, send = call(
        ortho_kernel,
        (shape(left.shape, bf16),) + (shape((width, HALF), f32),) * 2,
        where, gram_own, gram_other, left, mom_t, grad_t,
        scratch=ORTHO_SCRATCH,
    )
    part = enc(keep + swap(send), *RIGHT).reshape(nx, width // nx, HALF)
    mine = jnp.sum(dec(lax.all_to_all(part, "x", 0, 0), *RIGHT), axis=0)
    own = to_all(enc(mine, *RIGHT), "x", nx).reshape(width, HALF)
    other = swap(own)

    low = jnp.where(core == 0, own, other)
    high = jnp.where(core == 0, other, own)
    right = dec(jnp.concatenate([low, high], axis=1), *RIGHT)
    squares = jnp.sum(right * right, axis=0, keepdims=True)
    squares = to_all(squares, ZY, n).reshape(n, RANK)

    momentum_t = call(
        momentum_kernel,
        shape((width, left.shape[0]), f32),
        right, left_low, mom_t, grad_t,
    )
    factor_new, update_t = call(
        update_kernel,
        (shape((width, RANK), f32), shape((width, left.shape[0]), bf16)),
        right, left_low, squares,
    )
    return (momentum_t.T, factor_new, update_t.T)


def solution(mesh):
    nz = ny = math.isqrt(mesh.shape["fsdp"])
    nx = mesh.shape["tp"] // 2
    grid = Mesh(mesh.devices.reshape(nz, ny, nx, 2), ("z", "y", "x", "core"))
    tp = ("x", "core")
    return jax.shard_map(
        functools.partial(per_device, nz, ny, nx),
        mesh=grid,
        in_specs=(P(tp, ZY), P(tp, ZY), P(ZY, None)),
        out_specs=(P(tp, ZY), P(ZY, None), P(tp, ZY)),
        check_vma=False,
    )
```
